32 devices in a mesh: grp: 2 (over x), mod: 16 (over z, y, core).
Axes of the slice: x: 2, y: 2, z: 4, core: 2. Of those that a mesh axis runs over, the one named last changes fastest.
Arguments:
- inputs_proj: bfloat16 [128, 16, 1536], P(('grp', 'mod')), parts along dimension 0, may hold values from -2.5 to 2.5
- outputs_proj: bfloat16 [128, 16, 1280], P(('grp', 'mod')), parts along dimension 0, may hold values from -2.5 to 2.5
- lengths: int32 [128], P(('grp', 'mod')), parts along dimension 0, may hold values from 16 to 32, as said below
- owner: int32 [16], replicated, may hold values from 0 to 15, each once
- fisher_inv: bfloat16 [16, 1920, 1920], P('mod'), may hold values from -25 to 25, as said below
- query_grads: bfloat16 [16, 512, 1920], P('mod'), may hold values from -0.03125 to 0.03125
Outputs:
- scores: float32 [128, 512], P(('grp', 'mod')), parts along dimension 0
The draws below stay inside these ranges and needn't reach their ends.
There are 2 independent parts, one for each index of `grp`. The reference program is written for one: setup_inputs(seed, part) draws one part's arguments, and reference() takes and returns one part's arrays. A program takes and returns all parts, laid end to end along the dimension named above; an argument that names none is the same for every part. Nothing has to cross between parts.
Inputs may be any that keep to these rules, and one draw needn't show every extreme that they name: `fisher_inv`: each matrix is symmetric. `lengths`: some example of each group has all 32 slots live.
All inputs are finite; a program needn't handle non-finite values.
Results may differ from the reference program's by a relative error of at most 0.0041.
Values may be sent and summed in bfloat16 or wider, within the bound.
A program may use at most 128 MiB of HBM per device.

```python
import math
import jax
import jax.numpy as jnp
from jax import lax

OUT_RANK = 40
IN_RANK = 48
GRAD_DIM = 1920
SEQ_LEN = 32
QUERIES = 512
EXAMPLES = 64
MODULES = 16


def draw_lengths(key, part):
    key_len = jax.random.fold_in(key, 21)
    key_full = jax.random.fold_in(key, 22)
    drawn = jax.random.randint(key_len, (EXAMPLES,), SEQ_LEN // 2, SEQ_LEN + 1, dtype=jnp.int32)
    position = jax.random.randint(key_full, (), 0, EXAMPLES, dtype=jnp.int32)
    return jnp.where(jnp.arange(EXAMPLES, dtype=jnp.int32) == position, jnp.int32(SEQ_LEN), drawn)


def draw_fisher_inv(key, part):
    key_diag = jax.random.fold_in(key, 11)
    key_noise = jax.random.fold_in(key, 12)
    size = OUT_RANK * IN_RANK
    diag = jnp.exp(jax.random.uniform(key_diag, (MODULES, size), jnp.float32, math.log(0.5), math.log(2.0)))
    noise = jax.random.normal(key_noise, (MODULES, size, size), jnp.float32)
    noise = jnp.clip((noise + jnp.swapaxes(noise, 1, 2)) / math.sqrt(2.0), -6.0, 6.0)
    matrix = noise * (0.6 / math.sqrt(size)) + diag[:, :, None] * jnp.eye(size, dtype=jnp.float32)[None]
    return matrix.astype(jnp.bfloat16)


def level_of(rng, shape, cuts, smallest, largest):
    def one(dim, parts):
        steps = jax.random.uniform(jax.random.fold_in(jax.random.fold_in(rng, 6), dim), (parts,), jnp.float32, smallest / len(cuts), largest / len(cuts))
        return jnp.repeat(jnp.exp(steps), shape[dim] // parts).reshape((-1,) + (1,) * (len(shape) - dim - 1))

    level = one(*cuts[0])
    for cut in cuts[1:]:
        level = level * one(*cut)
    return level


def scatter_about(rng, shape, width, limit, pieces=(), kind=jnp.bfloat16):
    level = level_of(rng, shape, pieces, -0.22, 0.18) if pieces else 1.0
    result = jax.random.normal(rng, shape, jnp.float32) * width * level
    return jnp.minimum(jnp.maximum(result, -limit), limit).astype(kind)


def setup_inputs(seed: int = 0, part: int = 0) -> dict:
    key_list = jax.random.split(jax.random.key(seed), 7)
    part_keys = jax.random.split(jax.random.fold_in(key_list[6], part), 7)
    inputs_proj = scatter_about(part_keys[0], (EXAMPLES, MODULES, IN_RANK * SEQ_LEN), 0.4, 2.5, ((0, 16),))
    outputs_proj = scatter_about(part_keys[1], (EXAMPLES, MODULES, OUT_RANK * SEQ_LEN), 0.4, 2.5, ((0, 16),))
    lengths = draw_lengths(jax.random.fold_in(jax.random.fold_in(key_list[6], part), 71), part)
    owner = jax.random.permutation(key_list[3], MODULES).astype(jnp.int32)
    fisher_inv = draw_fisher_inv(jax.random.fold_in(key_list[6], 71), part)
    query_grads = scatter_about(key_list[5], (MODULES, QUERIES, GRAD_DIM), (GRAD_DIM * MODULES) ** -0.5, 0.03125, ((0, 16),))
    return dict(inputs_proj=inputs_proj, outputs_proj=outputs_proj, lengths=lengths, owner=owner, fisher_inv=fisher_inv, query_grads=query_grads)


def reference(inputs_proj, outputs_proj, lengths, owner, fisher_inv, query_grads):
    live = jnp.arange(SEQ_LEN, dtype=jnp.int32)[None, :] < lengths[:, None]
    live_in = jnp.where(live[:, None, None, :], inputs_proj.reshape(EXAMPLES, MODULES, IN_RANK, SEQ_LEN), jnp.zeros((), inputs_proj.dtype))
    live_out = jnp.where(live[:, None, None, :], outputs_proj.reshape(EXAMPLES, MODULES, OUT_RANK, SEQ_LEN), jnp.zeros((), outputs_proj.dtype))

    def one_module(total, index):
        feat_in = lax.dynamic_index_in_dim(live_in, index, 1, keepdims=False).astype(jnp.float32)
        feat_out = lax.dynamic_index_in_dim(live_out, index, 1, keepdims=False).astype(jnp.float32)
        grads = jnp.einsum("eol,eil->eoi", feat_out, feat_in).astype(jnp.bfloat16).reshape(EXAMPLES, OUT_RANK * IN_RANK)
        slot = owner[index]
        query_slot = lax.dynamic_index_in_dim(query_grads, slot, 0, keepdims=False)
        fisher_slot = lax.dynamic_index_in_dim(fisher_inv, slot, 0, keepdims=False)
        precond = jnp.dot(query_slot, fisher_slot, preferred_element_type=jnp.float32).astype(jnp.bfloat16)
        return total + jnp.dot(grads, precond.T, preferred_element_type=jnp.float32), None

    scores, _ = lax.scan(one_module, jnp.zeros((EXAMPLES, QUERIES), jnp.float32), jnp.arange(MODULES, dtype=jnp.int32))
    return scores
```

```python
import functools
import math

import jax
import jax.numpy as jnp
from jax import lax
from jax.experimental import pallas as pl
from jax.experimental.pallas import tpu as pltpu
from jax.sharding import PartitionSpec as P

MESH = pl.DeviceIdType.MESH
F32 = jnp.float32
BF16 = jnp.bfloat16
NT = (((1,), (1,)), ((), ()))

LANES = 128
WIDE = 256
PACK = 16
SUB = 8


def nt(a, b):
    return lax.dot_general(a, b, NT, preferred_element_type=F32)


def kernel(
    n,
    owner_ref,
    len_ref,
    in_ref,
    out_ref,
    f_hbm,
    q_hbm,
    res_ref,
    f_v,
    q_v,
    it_ref,
    ot_ref,
    gt_ref,
    p_ref,
    send_ref,
    recv_ref,
    rs_send,
    rs_recv,
    f_sem,
    q_sem,
    g_send_sem,
    g_recv_sem,
    s_send_sem,
    s_recv_sem,
):
    me = lax.axis_index("mod")
    rows = in_ref.shape[0]
    grad = f_hbm.shape[1]
    queries = q_hbm.shape[1]
    seq = math.isqrt(in_ref.shape[2] * out_ref.shape[2] // grad)
    rank_in = in_ref.shape[2] // seq
    rank_out = out_ref.shape[2] // seq
    quarters = PACK // rows
    outer = rank_out // quarters
    depth = outer * rank_in
    dests = WIDE // PACK
    groups = n // dests
    chunks_in = in_ref.shape[2] // WIDE
    chunks_out = out_ref.shape[2] // WIDE
    in_low = WIDE // seq
    out_low = WIDE // (seq * quarters)
    f_blocks = f_sem.shape[0]
    f_rows = grad // f_blocks

    def f_copy(b):
        where = pl.ds(b * f_rows, f_rows)
        return pltpu.make_async_copy(f_hbm.at[0, where], f_v.at[where], f_sem.at[b])

    q_copy = pltpu.make_async_copy(q_hbm.at[0], q_v, q_sem)
    q_copy.start()
    for b in range(f_blocks):
        f_copy(b).start()

    barrier = pltpu.get_barrier_semaphore()

    @pl.loop(1, n)
    def _(k):
        pl.semaphore_signal(
            barrier, inc=1, device_id={"mod": lax.rem(me + k, n)}, device_id_type=MESH
        )

    span = rows * n
    lane = lax.broadcasted_iota(jnp.int32, (1, span), 1)
    held = lax.fori_loop(
        0,
        n,
        lambda m, v: jnp.where(lax.rem(lane, n) == m, owner_ref[m], v),
        jnp.zeros((1, span), jnp.int32),
    )

    a = lax.broadcasted_iota(jnp.int32, (WIDE, WIDE), 0)
    b = lax.broadcasted_iota(jnp.int32, (WIDE, WIDE), 1)
    swap = ((a // in_low == b % seq) & (a % in_low == b // seq)).astype(BF16)
    eye = (a == b).astype(BF16)
    a = lax.broadcasted_iota(jnp.int32, (out_low * seq, WIDE), 0)
    b = lax.broadcasted_iota(jnp.int32, (out_low * seq, WIDE), 1)
    fold = ((a // seq == b // (seq * quarters)) & (a % seq == b % seq)).astype(BF16)

    a = lax.broadcasted_iota(jnp.int32, (WIDE, WIDE), 0)
    limit = jnp.zeros((WIDE, WIDE), jnp.int32)
    for e in range(rows):
        limit = jnp.where(a % rows == e, len_ref[e], limit)
    live = ((b_lane := lax.broadcasted_iota(jnp.int32, (WIDE, WIDE), 1)) % seq < limit) & (
        (b_lane // seq) % quarters == (a % PACK) // rows
    )

    gt_ref[pl.ds(depth, gt_ref.shape[0] - depth), :] = jnp.zeros(
        (gt_ref.shape[0] - depth, WIDE), F32
    )
    for s in range(quarters):
        p_ref[s, pl.ds(depth, p_ref.shape[1] - depth), :] = jnp.zeros(
            (p_ref.shape[1] - depth, queries), BF16
        )

    @pl.loop(0, groups)
    def _(g):
        row = lax.broadcasted_iota(jnp.int32, (WIDE, span), 0)
        col = lax.broadcasted_iota(jnp.int32, (WIDE, span), 1)
        pick = ((held == g * dests + row // PACK) & (col // n == row % rows)).astype(BF16)

        for c in range(chunks_in):
            x = in_ref[:, :, c * WIDE : (c + 1) * WIDE].reshape(span, WIDE)
            y = jnp.dot(pick, x, preferred_element_type=F32).astype(BF16)
            it_ref[c] = nt(swap, y)
        for c in range(chunks_out):
            x = out_ref[:, :, c * WIDE : (c + 1) * WIDE].reshape(span, WIDE)
            y = jnp.dot(pick, x, preferred_element_type=F32)
            y = jnp.where(live, y, 0.0).astype(BF16)
            ot_ref[pl.ds(c * out_low * seq, out_low * seq), :] = nt(fold, y)

        step = outer // 2
        for half in range(WIDE // LANES):
            at = pl.ds(half * LANES, LANES)
            for first in range(0, outer, step):

                def add(t8, acc):
                    acc = list(acc)
                    base = pl.multiple_of(t8 * SUB, SUB)
                    fos = [ot_ref[pl.ds((first + o) * seq + base, SUB), at] for o in range(step)]
                    for tt in range(SUB):
                        t = t8 * SUB + tt
                        fi = [
                            it_ref[c, pl.ds(pl.multiple_of(t * in_low, in_low), in_low), at]
                            for c in range(chunks_in)
                        ]
                        for o in range(step):
                            fo = fos[o][tt : tt + 1]
                            for c in range(chunks_in):
                                acc[o * chunks_in + c] = acc[o * chunks_in + c] + fi[c] * fo
                    return tuple(acc)

                acc = lax.fori_loop(
                    0,
                    seq // SUB,
                    add,
                    tuple(jnp.zeros((in_low, LANES), F32) for _ in range(step * chunks_in)),
                )
                for o in range(step):
                    for c in range(chunks_in):
                        gt_ref[pl.ds((first + o) * rank_in + c * in_low, in_low), at] = acc[
                            o * chunks_in + c
                        ]

        formed = nt(eye, gt_ref[...].astype(BF16)).astype(BF16)
        send_ref[pl.ds(g * dests, dests)] = formed.reshape(dests, PACK, formed.shape[1])

    pl.semaphore_wait(barrier, n - 1)

    def g_copy(dst, slot):
        return pltpu.make_async_remote_copy(
            src_ref=send_ref.at[dst],
            dst_ref=recv_ref.at[slot],
            send_sem=g_send_sem.at[dst],
            recv_sem=g_recv_sem.at[slot],
            device_id={"mod": dst},
            device_id_type=MESH,
        )

    def s_copy(dst, slot):
        return pltpu.make_async_remote_copy(
            src_ref=rs_send.at[dst],
            dst_ref=rs_recv.at[slot],
            send_sem=s_send_sem.at[dst],
            recv_sem=s_recv_sem.at[slot],
            device_id={"mod": dst},
            device_id_type=MESH,
        )

    @pl.loop(1, n)
    def _(k):
        g_copy(lax.rem(me + k, n), me).start()

    recv_ref[me] = send_ref[me]

    q_copy.wait()
    for blk in range(f_blocks):
        f_copy(blk).wait()
        part = nt(f_v[blk * f_rows : (blk + 1) * f_rows, :], q_v[...]).astype(BF16)
        for o in range(f_rows // rank_in):
            whole = blk * (f_rows // rank_in) + o
            p_ref[whole % quarters, pl.ds((whole // quarters) * rank_in, rank_in), :] = part[
                o * rank_in : (o + 1) * rank_in
            ]

    @pl.loop(1, n)
    def _(k):
        src = lax.rem(me + n - k, n)
        g_copy(src, src).wait_recv()

    @pl.loop(0, groups)
    def _(g):
        got = recv_ref[pl.ds(g * dests, dests)].reshape(WIDE, p_ref.shape[1])
        row = lax.broadcasted_iota(jnp.int32, got.shape, 0)
        total = jnp.zeros((WIDE, queries), F32)
        for s in range(quarters):
            mine = ((row % PACK) // rows == s).astype(F32).astype(BF16)
            total = total + jnp.dot(got * mine, p_ref[s], preferred_element_type=F32)
        total = total.reshape(dests, PACK, queries)
        total = total[:, :SUB] + total[:, SUB:]
        total = total + pltpu.roll(total, rows, 1)
        row = lax.broadcasted_iota(jnp.int32, (dests, SUB, queries // 2), 1)
        rs_send[pl.ds(g * dests, dests)] = jnp.where(
            row < rows, total[:, :, : queries // 2], total[:, :, queries // 2 :]
        )

    @pl.loop(1, n)
    def _(k):
        s_copy(lax.rem(me + k, n), me).start()

    rs_recv[me] = rs_send[me]

    @pl.loop(1, n)
    def _(k):
        src = lax.rem(me + n - k, n)
        s_copy(src, src).wait_recv()

    total = rs_recv[0]
    if n <= 32:
        for src in range(1, n):
            total = total + rs_recv[src]
    else:
        total = lax.fori_loop(1, n, lambda src, v: v + rs_recv[src], total)
    res_ref[:, : queries // 2] = total[:rows]
    res_ref[:, queries // 2 :] = total[rows:]

    @pl.loop(1, n)
    def _(k):
        dst = lax.rem(me + k, n)
        g_copy(dst, me).wait_send()
        s_copy(dst, me).wait_send()


def local(n, inputs_proj, outputs_proj, lengths, owner, fisher_inv, query_grads):
    rows = inputs_proj.shape[0]
    grad = fisher_inv.shape[1]
    queries = query_grads.shape[1]
    quarters = PACK // rows
    depth = grad // quarters
    padded = -(-depth // LANES) * LANES
    f_blocks = 4
    smem = pl.BlockSpec(memory_space=pltpu.SMEM)
    vmem = pl.BlockSpec(memory_space=pltpu.VMEM)
    hbm = pl.BlockSpec(memory_space=pl.ANY)
    return pl.pallas_call(
        functools.partial(kernel, n),
        out_shape=jax.ShapeDtypeStruct((rows, queries), F32),
        in_specs=[smem, smem, vmem, vmem, hbm, hbm],
        out_specs=vmem,
        scratch_shapes=[
            pltpu.VMEM((grad, grad), BF16),
            pltpu.VMEM((queries, grad), BF16),
            pltpu.VMEM((inputs_proj.shape[2] // WIDE, WIDE, WIDE), F32),
            pltpu.VMEM((outputs_proj.shape[2] // quarters, WIDE), F32),
            pltpu.VMEM((padded, WIDE), F32),
            pltpu.VMEM((quarters, padded, queries), BF16),
            pltpu.VMEM((n, PACK, padded), BF16),
            pltpu.VMEM((n, PACK, padded), BF16),
            pltpu.VMEM((n, SUB, queries // 2), F32),
            pltpu.VMEM((n, SUB, queries // 2), F32),
            pltpu.SemaphoreType.DMA((f_blocks,)),
            pltpu.SemaphoreType.DMA,
            pltpu.SemaphoreType.DMA((n,)),
            pltpu.SemaphoreType.DMA((n,)),
            pltpu.SemaphoreType.DMA((n,)),
            pltpu.SemaphoreType.DMA((n,)),
        ],
        compiler_params=pltpu.CompilerParams(
            collective_id=0, has_side_effects=True, vmem_limit_bytes=50 * 1024 * 1024
        ),
    )(owner, lengths, inputs_proj, outputs_proj, fisher_inv, query_grads)


def solution(mesh):
    return jax.shard_map(
        functools.partial(local, mesh.shape["mod"]),
        mesh=mesh,
        in_specs=(
            P(("grp", "mod"), None, None),
            P(("grp", "mod"), None, None),
            P(("grp", "mod")),
            P(),
            P("mod", None, None),
            P("mod", None, None),
        ),
        out_specs=P(("grp", "mod"), None),
        check_vma=False,
    )
```

```python
import functools
import math

import jax
import jax.numpy as jnp
from jax import lax
from jax.experimental import pallas as pl
from jax.experimental.pallas import tpu as pltpu
from jax.sharding import PartitionSpec as P

MESH = pl.DeviceIdType.MESH
F32 = jnp.float32
BF16 = jnp.bfloat16
NT = (((1,), (1,)), ((), ()))

LANES = 128
WIDE = 256
PACK = 16
SUB = 8
BLOCK = LANES // PACK


def nt(a, b):
    return lax.dot_general(a, b, NT, preferred_element_type=F32)


def over(a, k):
    return lax.shift_right_logical(a, k.bit_length() - 1) if k & (k - 1) == 0 else a // k


def mod(a, k):
    return lax.bitwise_and(a, k - 1) if k & (k - 1) == 0 else lax.rem(a, k)


def iota(shape, dim):
    return lax.broadcasted_iota(jnp.int32, shape, dim)


def kernel(
    n,
    owner_hbm,
    len_hbm,
    in_hbm,
    out_hbm,
    f_hbm,
    q_hbm,
    res_ref,
    owner_ref,
    len_ref,
    in_ref,
    out_ref,
    f_v,
    q_v,
    it_ref,
    ot_ref,
    gt_ref,
    p_ref,
    send_ref,
    recv_ref,
    rs_send,
    rs_recv,
    mine_ref,
    f_sem,
    small_sem,
    g_send_sem,
    g_recv_sem,
    s_send_sem,
    s_recv_sem,
):
    me = lax.axis_index("mod")
    rows = in_ref.shape[0]
    grad = f_hbm.shape[1]
    queries = q_hbm.shape[1]
    seq = math.isqrt(in_ref.shape[2] * out_ref.shape[2] // grad)
    rank_in = in_ref.shape[2] // seq
    rank_out = out_ref.shape[2] // seq
    quarters = PACK // rows
    outer = rank_out // quarters
    depth = outer * rank_in
    blocks = n // BLOCK
    chunks_in = in_ref.shape[2] // WIDE
    chunks_out = out_ref.shape[2] // WIDE
    in_low = WIDE // seq
    out_low = WIDE // (seq * quarters)
    f_blocks = f_sem.shape[0]
    f_rows = grad // f_blocks
    span = rows * n

    def f_copy(b):
        where = pl.ds(b * f_rows, f_rows)
        return pltpu.make_async_copy(f_hbm.at[0, where], f_v.at[where], f_sem.at[b])

    small = [
        pltpu.make_async_copy(src, dst, small_sem.at[i])
        for i, (src, dst) in enumerate(
            (
                (owner_hbm, owner_ref),
                (len_hbm, len_ref),
                (in_hbm, in_ref),
                (out_hbm, out_ref),
                (q_hbm.at[0], q_v),
            )
        )
    ]
    for copy in small:
        copy.start()
    for b in range(f_blocks):
        f_copy(b).start()

    barrier = pltpu.get_barrier_semaphore()

    @pl.loop(1, n)
    def _(k):
        pl.semaphore_signal(
            barrier, inc=1, device_id={"mod": lax.rem(me + k, n)}, device_id_type=MESH
        )

    a = iota((WIDE, WIDE), 0)
    b = iota((WIDE, WIDE), 1)
    swap = ((over(a, in_low) == mod(b, seq)) & (mod(a, in_low) == over(b, seq))).astype(BF16)
    a = iota((out_low * seq, WIDE), 0)
    b = iota((out_low * seq, WIDE), 1)
    fold = ((over(a, seq) == over(b, seq * quarters)) & (mod(a, seq) == mod(b, seq))).astype(BF16)
    eye = (iota((LANES, LANES), 0) == iota((LANES, LANES), 1)).astype(BF16)

    gt_ref[pl.ds(depth, gt_ref.shape[0] - depth), :] = jnp.zeros(
        (gt_ref.shape[0] - depth, LANES), F32
    )
    for s in range(quarters):
        p_ref[s, pl.ds(depth, p_ref.shape[1] - depth), :] = jnp.zeros(
            (p_ref.shape[1] - depth, queries), BF16
        )

    for copy in small[:2]:
        copy.wait()

    lane = mod(iota((1, span), 1), n)
    held = jnp.zeros((1, span), jnp.int32)
    if n <= 32:
        for m in range(n):
            held = jnp.where(lane == m, owner_ref[m], held)
    else:
        held = lax.fori_loop(
            0, n, lambda m, v: jnp.where(lane == m, owner_ref[m], v), held
        )

    a = iota((LANES, WIDE), 0)
    b = iota((LANES, WIDE), 1)
    limit = jnp.zeros((LANES, WIDE), jnp.int32)
    for e in range(rows):
        limit = jnp.where(mod(a, rows) == e, len_ref[e], limit)
    live = (mod(b, seq) < limit) & (mod(over(b, seq), quarters) == over(mod(a, PACK), rows))

    for copy in small[2:4]:
        copy.wait()

    def block_at(p):
        return lax.rem(over(me, BLOCK) + 1 + p, blocks)

    def peer(p, s):
        return block_at(p) * BLOCK + mod(me + s, BLOCK)

    def g_copy(dst, slot):
        return pltpu.make_async_remote_copy(
            src_ref=send_ref.at[dst],
            dst_ref=recv_ref.at[slot],
            send_sem=g_send_sem.at[dst],
            recv_sem=g_recv_sem.at[slot],
            device_id={"mod": dst},
            device_id_type=MESH,
        )

    def s_copy(dst, slot):
        return pltpu.make_async_remote_copy(
            src_ref=rs_send.at[dst],
            dst_ref=rs_recv.at[slot],
            send_sem=s_send_sem.at[dst],
            recv_sem=s_recv_sem.at[slot],
            device_id={"mod": dst},
            device_id_type=MESH,
        )

    @pl.loop(0, blocks)
    def _(p):
        row = iota((LANES, span), 0)
        col = iota((LANES, span), 1)
        pick = (
            (held == block_at(p) * BLOCK + over(row, PACK)) & (over(col, n) == mod(row, rows))
        ).astype(BF16)

        for c in range(chunks_out):
            x = out_ref[:, :, c * WIDE : (c + 1) * WIDE].reshape(span, WIDE)
            y = jnp.dot(pick, x, preferred_element_type=F32)
            y = jnp.where(live, y, 0.0).astype(BF16)
            ot_ref[pl.ds(c * out_low * seq, out_low * seq), :] = nt(fold, y)
        for c in range(chunks_in):
            x = in_ref[:, :, c * WIDE : (c + 1) * WIDE].reshape(span, WIDE)
            y = jnp.dot(pick, x, preferred_element_type=F32).astype(BF16)
            it_ref[c] = nt(swap, y)

        step = outer // 2
        for first in range(0, outer, step):

            def add(t8, acc):
                acc = list(acc)
                base = pl.multiple_of(t8 * SUB, SUB)
                fos = [ot_ref[pl.ds((first + o) * seq + base, SUB), :] for o in range(step)]
                for tt in range(SUB):
                    t = t8 * SUB + tt
                    fi = [
                        it_ref[c, pl.ds(pl.multiple_of(t * in_low, in_low), in_low), :]
                        for c in range(chunks_in)
                    ]
                    for o in range(step):
                        fo = fos[o][tt : tt + 1]
                        for c in range(chunks_in):
                            acc[o * chunks_in + c] = acc[o * chunks_in + c] + fi[c] * fo
                return tuple(acc)

            acc = lax.fori_loop(
                0,
                seq // SUB,
                add,
                tuple(jnp.zeros((in_low, LANES), F32) for _ in range(step * chunks_in)),
            )
            for o in range(step):
                for c in range(chunks_in):
                    gt_ref[pl.ds((first + o) * rank_in + c * in_low, in_low), :] = acc[
                        o * chunks_in + c
                    ]

        formed = nt(eye, gt_ref[...].astype(BF16)).astype(BF16)
        send_ref[pl.ds(block_at(p) * BLOCK, BLOCK)] = formed.reshape(
            BLOCK, PACK, formed.shape[1]
        )

        @pl.when(p == 0)
        def _():
            pl.semaphore_wait(barrier, n - 1)

        @pl.loop(0, BLOCK)
        def _(s):
            dst = peer(p, s)

            @pl.when(dst != me)
            def _():
                g_copy(dst, me).start()

    recv_ref[me] = send_ref[me]

    small[4].wait()
    for blk in range(f_blocks):
        f_copy(blk).wait()
        part = nt(f_v[blk * f_rows : (blk + 1) * f_rows, :], q_v[...]).astype(BF16)
        for o in range(f_rows // rank_in):
            whole = blk * (f_rows // rank_in) + o
            p_ref[whole % quarters, pl.ds((whole // quarters) * rank_in, rank_in), :] = part[
                o * rank_in : (o + 1) * rank_in
            ]

    @pl.loop(0, blocks)
    def _(back):
        p = blocks - 1 - back

        @pl.loop(0, BLOCK)
        def _(s):
            src = peer(p, s)

            @pl.when(src != me)
            def _():
                g_copy(src, src).wait_recv()

        got = recv_ref[pl.ds(block_at(p) * BLOCK, BLOCK)].reshape(LANES, p_ref.shape[1])
        row = iota(got.shape, 0)
        total = jnp.zeros((LANES, queries), F32)
        for s in range(quarters):
            mine = (over(mod(row, PACK), rows) == s).astype(F32).astype(BF16)
            total = total + jnp.dot(got * mine, p_ref[s], preferred_element_type=F32)
        total = total.reshape(BLOCK, PACK, queries)
        total = total[:, :SUB] + total[:, SUB:]
        total = total + pltpu.roll(total, rows, 1)
        width = queries // quarters
        low = iota((BLOCK, SUB, width), 1) < rows
        pieces = [
            jnp.where(
                low,
                total[:, :, 2 * i * width : (2 * i + 1) * width],
                total[:, :, (2 * i + 1) * width : (2 * i + 2) * width],
            )
            for i in range(quarters // 2)
        ]
        total = jnp.concatenate(pieces, axis=1)
        mine_ref[pl.ds(block_at(p) * BLOCK, BLOCK)] = total
        rs_send[pl.ds(block_at(p) * BLOCK, BLOCK)] = total.astype(BF16)

        @pl.loop(0, BLOCK)
        def _(s):
            dst = peer(p, s)

            @pl.when(dst != me)
            def _():
                s_copy(dst, me).start()

    rs_recv[me] = jnp.zeros(rs_recv.shape[1:], BF16)

    @pl.loop(1, n)
    def _(k):
        src = lax.rem(me + n - k, n)
        s_copy(src, src).wait_recv()

    total = mine_ref[me]
    if n <= 32:
        for src in range(n):
            total = total + rs_recv[src].astype(F32)
    else:
        total = lax.fori_loop(0, n, lambda src, v: v + rs_recv[src].astype(F32), total)
    width = queries // quarters
    for s in range(quarters):
        res_ref[:, s * width : (s + 1) * width] = total[s * rows : (s + 1) * rows]

    @pl.loop(1, n)
    def _(k):
        dst = lax.rem(me + k, n)
        g_copy(dst, me).wait_send()
        s_copy(dst, me).wait_send()


def local(n, inputs_proj, outputs_proj, lengths, owner, fisher_inv, query_grads):
    rows = inputs_proj.shape[0]
    grad = fisher_inv.shape[1]
    queries = query_grads.shape[1]
    quarters = PACK // rows
    depth = grad // quarters
    padded = -(-depth // LANES) * LANES
    f_blocks = 4
    return pl.pallas_call(
        functools.partial(kernel, n),
        out_shape=jax.ShapeDtypeStruct((rows, queries), F32),
        in_specs=[pl.BlockSpec(memory_space=pltpu.HBM)] * 6,
        out_specs=pl.BlockSpec(memory_space=pltpu.VMEM),
        scratch_shapes=[
            pltpu.SMEM(owner.shape, jnp.int32),
            pltpu.SMEM(lengths.shape, jnp.int32),
            pltpu.VMEM(inputs_proj.shape, BF16),
            pltpu.VMEM(outputs_proj.shape, BF16),
            pltpu.VMEM((grad, grad), BF16),
            pltpu.VMEM((queries, grad), BF16),
            pltpu.VMEM((inputs_proj.shape[2] // WIDE, WIDE, LANES), F32),
            pltpu.VMEM((outputs_proj.shape[2] // quarters, LANES), F32),
            pltpu.VMEM((padded, LANES), F32),
            pltpu.VMEM((quarters, padded, queries), BF16),
            pltpu.VMEM((n, PACK, padded), BF16),
            pltpu.VMEM((n, PACK, padded), BF16),
            pltpu.VMEM((n, PACK, queries // quarters), BF16),
            pltpu.VMEM((n, PACK, queries // quarters), BF16),
            pltpu.VMEM((n, PACK, queries // quarters), F32),
            pltpu.SemaphoreType.DMA((f_blocks,)),
            pltpu.SemaphoreType.DMA((5,)),
            pltpu.SemaphoreType.DMA((n,)),
            pltpu.SemaphoreType.DMA((n,)),
            pltpu.SemaphoreType.DMA((n,)),
            pltpu.SemaphoreType.DMA((n,)),
        ],
        compiler_params=pltpu.CompilerParams(
            collective_id=0, has_side_effects=True, vmem_limit_bytes=64 * 1024 * 1024
        ),
    )(owner, lengths, inputs_proj, outputs_proj, fisher_inv, query_grads)


def solution(mesh):
    return jax.shard_map(
        functools.partial(local, mesh.shape["mod"]),
        mesh=mesh,
        in_specs=(
            P(("grp", "mod"), None, None),
            P(("grp", "mod"), None, None),
            P(("grp", "mod")),
            P(),
            P("mod", None, None),
            P("mod", None, None),
        ),
        out_specs=P(("grp", "mod"), None),
        check_vma=False,
    )
```

```python
import functools
import math

import jax
import jax.numpy as jnp
from jax import lax
from jax.experimental import pallas as pl
from jax.experimental.pallas import tpu as pltpu
from jax.sharding import PartitionSpec as P

MESH = pl.DeviceIdType.MESH
F32 = jnp.float32
BF16 = jnp.bfloat16
NT = (((1,), (1,)), ((), ()))

LANES = 128
WIDE = 256
PACK = 16
SUB = 8
BLOCK = LANES // PACK


def nt(a, b):
    return lax.dot_general(a, b, NT, preferred_element_type=F32)


def over(a, k):
    return lax.shift_right_logical(a, k.bit_length() - 1) if k & (k - 1) == 0 else a // k


def mod(a, k):
    return lax.bitwise_and(a, k - 1) if k & (k - 1) == 0 else lax.rem(a, k)


def each(low, high, body, most=16):
    if high - low <= most:
        for k in range(low, high):
            body(k)
    else:
        pl.loop(low, high)(body)


def iota(shape, dim):
    return lax.broadcasted_iota(jnp.int32, shape, dim)


def kernel(
    n,
    owner_hbm,
    len_hbm,
    in_hbm,
    out_hbm,
    f_hbm,
    q_hbm,
    res_ref,
    owner_ref,
    len_ref,
    in_ref,
    out_ref,
    f_v,
    q_v,
    it_ref,
    ot_ref,
    gt_ref,
    p_ref,
    send_ref,
    recv_ref,
    rs_send,
    rs_recv,
    mine_ref,
    f_sem,
    small_sem,
    g_send_sem,
    g_recv_sem,
    s_send_sem,
    s_recv_sem,
):
    me = lax.axis_index("mod")
    rows = in_ref.shape[0]
    grad = f_hbm.shape[1]
    queries = q_hbm.shape[1]
    seq = math.isqrt(in_ref.shape[2] * out_ref.shape[2] // grad)
    rank_in = in_ref.shape[2] // seq
    rank_out = out_ref.shape[2] // seq
    quarters = PACK // rows
    outer = rank_out // quarters
    depth = outer * rank_in
    blocks = n // BLOCK
    chunks_in = in_ref.shape[2] // WIDE
    chunks_out = out_ref.shape[2] // WIDE
    in_low = WIDE // seq
    out_low = WIDE // (seq * quarters)
    f_blocks = f_sem.shape[0]
    f_rows = grad // f_blocks
    span = rows * n

    def f_copy(b):
        where = pl.ds(b * f_rows, f_rows)
        return pltpu.make_async_copy(f_hbm.at[0, where], f_v.at[where], f_sem.at[b])

    small = [
        pltpu.make_async_copy(src, dst, small_sem.at[i])
        for i, (src, dst) in enumerate(
            (
                (owner_hbm, owner_ref),
                (len_hbm, len_ref),
                (in_hbm, in_ref),
                (out_hbm, out_ref),
                (q_hbm.at[0], q_v),
            )
        )
    ]
    for copy in small:
        copy.start()
    for b in range(f_blocks):
        f_copy(b).start()

    barrier = pltpu.get_barrier_semaphore()

    def greet(k):
        pl.semaphore_signal(
            barrier, inc=1, device_id={"mod": mod(me + k, n)}, device_id_type=MESH
        )

    each(1, n, greet)

    a = iota((WIDE, WIDE), 0)
    b = iota((WIDE, WIDE), 1)
    swap = ((over(a, in_low) == mod(b, seq)) & (mod(a, in_low) == over(b, seq))).astype(BF16)
    a = iota((out_low * seq, WIDE), 0)
    b = iota((out_low * seq, WIDE), 1)
    fold = ((over(a, seq) == over(b, seq * quarters)) & (mod(a, seq) == mod(b, seq))).astype(BF16)
    eye = (iota((LANES, LANES), 0) == iota((LANES, LANES), 1)).astype(BF16)

    gt_ref[pl.ds(depth, gt_ref.shape[0] - depth), :] = jnp.zeros(
        (gt_ref.shape[0] - depth, LANES), F32
    )
    for s in range(quarters):
        p_ref[s, pl.ds(depth, p_ref.shape[1] - depth), :] = jnp.zeros(
            (p_ref.shape[1] - depth, queries), BF16
        )

    for copy in small[:2]:
        copy.wait()

    lane = mod(iota((1, span), 1), n)
    held = jnp.zeros((1, span), jnp.int32)
    if n <= 32:
        for m in range(n):
            held = jnp.where(lane == m, owner_ref[m], held)
    else:
        held = lax.fori_loop(
            0, n, lambda m, v: jnp.where(lane == m, owner_ref[m], v), held
        )

    a = iota((LANES, WIDE), 0)
    b = iota((LANES, WIDE), 1)
    limit = jnp.zeros((LANES, WIDE), jnp.int32)
    for e in range(rows):
        limit = jnp.where(mod(a, rows) == e, len_ref[e], limit)
    live = (mod(b, seq) < limit) & (mod(over(b, seq), quarters) == over(mod(a, PACK), rows))

    for copy in small[2:4]:
        copy.wait()

    def block_at(p):
        return mod(over(me, BLOCK) + 1 + p, blocks)

    def peer(p, s):
        return block_at(p) * BLOCK + mod(me + s, BLOCK)

    def g_copy(dst):
        return pltpu.make_async_remote_copy(
            src_ref=send_ref.at[dst],
            dst_ref=recv_ref.at[me],
            send_sem=g_send_sem,
            recv_sem=g_recv_sem.at[over(me, BLOCK)],
            device_id={"mod": dst},
            device_id_type=MESH,
        )

    def s_copy(dst):
        return pltpu.make_async_remote_copy(
            src_ref=rs_send.at[dst],
            dst_ref=rs_recv.at[me],
            send_sem=s_send_sem,
            recv_sem=s_recv_sem,
            device_id={"mod": dst},
            device_id_type=MESH,
        )

    def wait_for(ref, count, sem):
        part = ref.at[pl.ds(0, count)]
        pltpu.make_async_copy(part, part, sem).wait()

    def form(p, own):
        row = iota((LANES, span), 0)
        col = iota((LANES, span), 1)
        pick = (
            (held == block_at(p) * BLOCK + over(row, PACK)) & (over(col, n) == mod(row, rows))
        ).astype(BF16)

        for c in range(chunks_out):
            x = out_ref[:, :, c * WIDE : (c + 1) * WIDE].reshape(span, WIDE)
            y = jnp.dot(pick, x, preferred_element_type=F32)
            y = jnp.where(live, y, 0.0).astype(BF16)
            ot_ref[pl.ds(c * out_low * seq, out_low * seq), :] = nt(fold, y)
        for c in range(chunks_in):
            x = in_ref[:, :, c * WIDE : (c + 1) * WIDE].reshape(span, WIDE)
            y = jnp.dot(pick, x, preferred_element_type=F32).astype(BF16)
            it_ref[c] = nt(swap, y)

        step = outer // 2
        for first in range(0, outer, step):

            acc = [jnp.zeros((in_low, LANES), F32)] * (step * chunks_in)
            for t in range(seq):
                fi = [it_ref[c, t * in_low : (t + 1) * in_low, :] for c in range(chunks_in)]
                for o in range(step):
                    fo = ot_ref[(first + o) * seq + t : (first + o) * seq + t + 1, :]
                    for c in range(chunks_in):
                        acc[o * chunks_in + c] = acc[o * chunks_in + c] + fi[c] * fo
            for o in range(step):
                for c in range(chunks_in):
                    gt_ref[pl.ds((first + o) * rank_in + c * in_low, in_low), :] = acc[
                        o * chunks_in + c
                    ]

        formed = nt(eye, gt_ref[...].astype(BF16)).astype(BF16)
        send_ref[pl.ds(block_at(p) * BLOCK, BLOCK)] = formed.reshape(
            BLOCK, PACK, formed.shape[1]
        )

        if own:
            each(1, BLOCK, lambda s: g_copy(peer(p, s)).start())
        else:
            each(0, BLOCK, lambda s: g_copy(peer(p, s)).start())

    pl.semaphore_wait(barrier, n - 1)
    each(0, blocks - 1, lambda p: form(p, False), 2)
    form(blocks - 1, True)
    recv_ref[me] = send_ref[me]

    small[4].wait()
    for blk in range(f_blocks):
        f_copy(blk).wait()
        part = nt(f_v[blk * f_rows : (blk + 1) * f_rows, :], q_v[...]).astype(BF16)
        for o in range(f_rows // rank_in):
            whole = blk * (f_rows // rank_in) + o
            p_ref[whole % quarters, pl.ds((whole // quarters) * rank_in, rank_in), :] = part[
                o * rank_in : (o + 1) * rank_in
            ]

    def score(p, own):
        wait_for(recv_ref, BLOCK - 1 if own else BLOCK, g_recv_sem.at[block_at(p)])
        got = recv_ref[pl.ds(block_at(p) * BLOCK, BLOCK)].reshape(LANES, p_ref.shape[1])
        row = iota(got.shape, 0)
        total = jnp.zeros((LANES, queries), F32)
        for s in range(quarters):
            mine = (over(mod(row, PACK), rows) == s).astype(F32).astype(BF16)
            total = total + jnp.dot(got * mine, p_ref[s], preferred_element_type=F32)
        total = total.reshape(BLOCK, PACK, queries)
        total = total[:, :SUB] + total[:, SUB:]
        total = total + pltpu.roll(total, rows, 1)
        width = queries // quarters
        low = iota((BLOCK, SUB, width), 1) < rows
        pieces = [
            jnp.where(
                low,
                total[:, :, 2 * i * width : (2 * i + 1) * width],
                total[:, :, (2 * i + 1) * width : (2 * i + 2) * width],
            )
            for i in range(quarters // 2)
        ]
        total = jnp.concatenate(pieces, axis=1)
        mine_ref[pl.ds(block_at(p) * BLOCK, BLOCK)] = total
        rs_send[pl.ds(block_at(p) * BLOCK, BLOCK)] = total.astype(BF16)

        if own:
            each(1, BLOCK, lambda s: s_copy(peer(p, s)).start())
        else:
            each(0, BLOCK, lambda s: s_copy(peer(p, s)).start())

    score(blocks - 1, True)
    each(0, blocks - 1, lambda p: score(p, False), 2)
    rs_recv[me] = jnp.zeros(rs_recv.shape[1:], BF16)
    wait_for(rs_recv, n - 1, s_recv_sem)

    total = mine_ref[me]
    if n <= 32:
        for src in range(n):
            total = total + rs_recv[src].astype(F32)
    else:
        total = lax.fori_loop(0, n, lambda src, v: v + rs_recv[src].astype(F32), total)
    width = queries // quarters
    for s in range(quarters):
        res_ref[:, s * width : (s + 1) * width] = total[s * rows : (s + 1) * rows]

    wait_for(send_ref, n - 1, g_send_sem)
    wait_for(rs_send, n - 1, s_send_sem)


def local(n, inputs_proj, outputs_proj, lengths, owner, fisher_inv, query_grads):
    rows = inputs_proj.shape[0]
    grad = fisher_inv.shape[1]
    queries = query_grads.shape[1]
    quarters = PACK // rows
    depth = grad // quarters
    padded = -(-depth // LANES) * LANES
    f_blocks = 4
    return pl.pallas_call(
        functools.partial(kernel, n),
        out_shape=jax.ShapeDtypeStruct((rows, queries), F32),
        in_specs=[pl.BlockSpec(memory_space=pltpu.HBM)] * 6,
        out_specs=pl.BlockSpec(memory_space=pltpu.VMEM),
        scratch_shapes=[
            pltpu.SMEM(owner.shape, jnp.int32),
            pltpu.SMEM(lengths.shape, jnp.int32),
            pltpu.VMEM(inputs_proj.shape, BF16),
            pltpu.VMEM(outputs_proj.shape, BF16),
            pltpu.VMEM((grad, grad), BF16),
            pltpu.VMEM((queries, grad), BF16),
            pltpu.VMEM((inputs_proj.shape[2] // WIDE, WIDE, LANES), F32),
            pltpu.VMEM((outputs_proj.shape[2] // quarters, LANES), F32),
            pltpu.VMEM((padded, LANES), F32),
            pltpu.VMEM((quarters, padded, queries), BF16),
            pltpu.VMEM((n, PACK, padded), BF16),
            pltpu.VMEM((n, PACK, padded), BF16),
            pltpu.VMEM((n, PACK, queries // quarters), BF16),
            pltpu.VMEM((n, PACK, queries // quarters), BF16),
            pltpu.VMEM((n, PACK, queries // quarters), F32),
            pltpu.SemaphoreType.DMA((f_blocks,)),
            pltpu.SemaphoreType.DMA((5,)),
            pltpu.SemaphoreType.DMA,
            pltpu.SemaphoreType.DMA((n // BLOCK,)),
            pltpu.SemaphoreType.DMA,
            pltpu.SemaphoreType.DMA,
        ],
        compiler_params=pltpu.CompilerParams(
            collective_id=0, has_side_effects=True, vmem_limit_bytes=64 * 1024 * 1024
        ),
    )(owner, lengths, inputs_proj, outputs_proj, fisher_inv, query_grads)


def solution(mesh):
    return jax.shard_map(
        functools.partial(local, mesh.shape["mod"]),
        mesh=mesh,
        in_specs=(
            P(("grp", "mod"), None, None),
            P(("grp", "mod"), None, None),
            P(("grp", "mod")),
            P(),
            P("mod", None, None),
            P("mod", None, None),
        ),
        out_specs=P(("grp", "mod"), None),
        check_vma=False,
    )
```

```python
import functools
import math

import jax
import jax.numpy as jnp
from jax import lax
from jax.experimental import pallas as pl
from jax.experimental.pallas import tpu as pltpu
from jax.sharding import PartitionSpec as P

MESH = pl.DeviceIdType.MESH
F32 = jnp.float32
BF16 = jnp.bfloat16
NT = (((1,), (1,)), ((), ()))

LANES = 128
WIDE = 256
PACK = 16
SUB = 8
BLOCK = LANES // PACK
PLANE = BLOCK // 2


def nt(a, b):
    return lax.dot_general(a, b, NT, preferred_element_type=F32)


def over(a, k):
    return lax.shift_right_logical(a, k.bit_length() - 1) if k & (k - 1) == 0 else a // k


def mod(a, k):
    return lax.bitwise_and(a, k - 1) if k & (k - 1) == 0 else lax.rem(a, k)


def each(low, high, body, most=16):
    if high - low <= most:
        for k in range(low, high):
            body(k)
    else:
        pl.loop(low, high)(body)


def iota(shape, dim):
    return lax.broadcasted_iota(jnp.int32, shape, dim)


def kernel(
    n,
    owner_hbm,
    len_hbm,
    in_hbm,
    out_hbm,
    f_hbm,
    q_hbm,
    res_ref,
    owner_ref,
    len_ref,
    in_ref,
    out_ref,
    f_v,
    q_v,
    it_ref,
    ot_ref,
    gt_ref,
    p_ref,
    send_ref,
    recv_ref,
    rs_send,
    rs_recv,
    mine_ref,
    f_sem,
    small_sem,
    g_send_sem,
    g_recv_sem,
    s_send_sem,
    s_recv_sem,
):
    me = lax.axis_index("mod")
    rows = in_ref.shape[0]
    grad = f_hbm.shape[1]
    queries = q_hbm.shape[1]
    seq = math.isqrt(in_ref.shape[2] * out_ref.shape[2] // grad)
    rank_in = in_ref.shape[2] // seq
    rank_out = out_ref.shape[2] // seq
    quarters = PACK // rows
    outer = rank_out // quarters
    depth = outer * rank_in
    blocks = n // BLOCK
    chunks_in = in_ref.shape[2] // WIDE
    chunks_out = out_ref.shape[2] // WIDE
    in_low = WIDE // seq
    out_low = WIDE // (seq * quarters)
    f_blocks = f_sem.shape[0]
    f_rows = grad // f_blocks
    span = rows * n

    def f_copy(b):
        where = pl.ds(b * f_rows, f_rows)
        return pltpu.make_async_copy(f_hbm.at[0, where], f_v.at[where], f_sem.at[b])

    small = [
        pltpu.make_async_copy(src, dst, small_sem.at[i])
        for i, (src, dst) in enumerate(
            (
                (owner_hbm, owner_ref),
                (len_hbm, len_ref),
                (in_hbm, in_ref),
                (out_hbm, out_ref),
                (q_hbm.at[0], q_v),
            )
        )
    ]
    for copy in small:
        copy.start()
    for b in range(f_blocks):
        f_copy(b).start()

    barrier = pltpu.get_barrier_semaphore()

    def greet(k):
        pl.semaphore_signal(
            barrier, inc=1, device_id={"mod": mod(me + k, n)}, device_id_type=MESH
        )

    each(1, n, greet)

    a = iota((WIDE, WIDE), 0)
    b = iota((WIDE, WIDE), 1)
    swap = ((over(a, in_low) == mod(b, seq)) & (mod(a, in_low) == over(b, seq))).astype(BF16)
    a = iota((out_low * seq, WIDE), 0)
    b = iota((out_low * seq, WIDE), 1)
    fold = ((over(a, seq) == over(b, seq * quarters)) & (mod(a, seq) == mod(b, seq))).astype(BF16)
    eye = (iota((LANES, LANES), 0) == iota((LANES, LANES), 1)).astype(BF16)

    gt_ref[pl.ds(depth, gt_ref.shape[0] - depth), :] = jnp.zeros(
        (gt_ref.shape[0] - depth, LANES), F32
    )
    for s in range(quarters):
        p_ref[s, pl.ds(depth, p_ref.shape[1] - depth), :] = jnp.zeros(
            (p_ref.shape[1] - depth, queries), BF16
        )

    for copy in small[:2]:
        copy.wait()

    lane = mod(iota((1, span), 1), n)
    held = jnp.zeros((1, span), jnp.int32)
    if n <= 32:
        for m in range(n):
            held = jnp.where(lane == m, owner_ref[m], held)
    else:
        held = lax.fori_loop(
            0, n, lambda m, v: jnp.where(lane == m, owner_ref[m], v), held
        )

    a = iota((LANES, WIDE), 0)
    b = iota((LANES, WIDE), 1)
    limit = jnp.zeros((LANES, WIDE), jnp.int32)
    for e in range(rows):
        limit = jnp.where(mod(a, rows) == e, len_ref[e], limit)
    live = (mod(b, seq) < limit) & (mod(over(b, seq), quarters) == over(mod(a, PACK), rows))

    for copy in small[2:4]:
        copy.wait()

    def block_at(p):
        return mod(over(me, BLOCK) + 1 + p, blocks)

    def plane_at(p, h):
        return block_at(p) * 2 + mod(over(me, PLANE) + h, 2)

    def peer(p, h, s):
        return plane_at(p, h) * PLANE + mod(me + s, PLANE)

    def peers(p, own):
        return [
            peer(p, h, s) for h in range(2) for s in range(1 if own and h == 0 else 0, PLANE)
        ]

    def precondition(blk):
        part = nt(f_v[blk * f_rows : (blk + 1) * f_rows, :], q_v[...]).astype(BF16)
        for o in range(f_rows // rank_in):
            whole = blk * (f_rows // rank_in) + o
            p_ref[whole % quarters, pl.ds((whole // quarters) * rank_in, rank_in), :] = part[
                o * rank_in : (o + 1) * rank_in
            ]

    def g_copy(dst):
        return pltpu.make_async_remote_copy(
            src_ref=send_ref.at[dst],
            dst_ref=recv_ref.at[me],
            send_sem=g_send_sem,
            recv_sem=g_recv_sem.at[over(me, PLANE)],
            device_id={"mod": dst},
            device_id_type=MESH,
        )

    def s_copy(dst):
        return pltpu.make_async_remote_copy(
            src_ref=rs_send.at[dst],
            dst_ref=rs_recv.at[me],
            send_sem=s_send_sem,
            recv_sem=s_recv_sem,
            device_id={"mod": dst},
            device_id_type=MESH,
        )

    def wait_for(ref, count, sem):
        part = ref.at[pl.ds(0, count)]
        pltpu.make_async_copy(part, part, sem).wait()

    def form(p, own):
        if own:
            small[4].wait()
            for blk in range(early):
                f_copy(blk).wait()
        row = iota((LANES, span), 0)
        col = iota((LANES, span), 1)
        pick = (
            (held == block_at(p) * BLOCK + over(row, PACK)) & (over(col, n) == mod(row, rows))
        ).astype(BF16)

        for c in range(chunks_out):
            x = out_ref[:, :, c * WIDE : (c + 1) * WIDE].reshape(span, WIDE)
            y = jnp.dot(pick, x, preferred_element_type=F32)
            y = jnp.where(live, y, 0.0).astype(BF16)
            ot_ref[pl.ds(c * out_low * seq, out_low * seq), :] = nt(fold, y)
        for c in range(chunks_in):
            x = in_ref[:, :, c * WIDE : (c + 1) * WIDE].reshape(span, WIDE)
            y = jnp.dot(pick, x, preferred_element_type=F32).astype(BF16)
            it_ref[c] = nt(swap, y)

        step = outer // 2
        for first in range(0, outer, step):
            if own:
                precondition(first // step)
            acc = [jnp.zeros((in_low, LANES), F32)] * (step * chunks_in)
            for t in range(seq):
                fi = [it_ref[c, t * in_low : (t + 1) * in_low, :] for c in range(chunks_in)]
                for o in range(step):
                    fo = ot_ref[(first + o) * seq + t : (first + o) * seq + t + 1, :]
                    for c in range(chunks_in):
                        acc[o * chunks_in + c] = acc[o * chunks_in + c] + fi[c] * fo
            for o in range(step):
                for c in range(chunks_in):
                    gt_ref[pl.ds((first + o) * rank_in + c * in_low, in_low), :] = acc[
                        o * chunks_in + c
                    ]

        formed = nt(eye, gt_ref[...].astype(BF16)).astype(BF16)
        send_ref[pl.ds(block_at(p) * BLOCK, BLOCK)] = formed.reshape(
            BLOCK, PACK, formed.shape[1]
        )

        if isinstance(p, int):
            if p == 0:
                pl.semaphore_wait(barrier, n - 1)
        else:
            pl.when(p == 0)(lambda: pl.semaphore_wait(barrier, n - 1))
        for dst in peers(p, own):
            g_copy(dst).start()

    early = 2
    each(0, blocks - 1, lambda p: form(p, False), 2)
    form(blocks - 1, True)
    recv_ref[me] = send_ref[me]

    for blk in range(early, f_blocks):
        f_copy(blk).wait()
        precondition(blk)

    def score(p, own, halves):
        count = len(halves) * PLANE
        for h in halves:
            wait_for(
                recv_ref, PLANE - 1 if own and h == 0 else PLANE, g_recv_sem.at[plane_at(p, h)]
            )
        start = block_at(p) * BLOCK if len(halves) == 2 else plane_at(p, halves[0]) * PLANE
        got = recv_ref[pl.ds(start, count)].reshape(count * PACK, p_ref.shape[1])
        row = iota(got.shape, 0)
        total = jnp.zeros((count * PACK, queries), F32)
        for s in range(quarters):
            mine = (over(mod(row, PACK), rows) == s).astype(F32).astype(BF16)
            total = total + jnp.dot(got * mine, p_ref[s], preferred_element_type=F32)
        total = total.reshape(count, PACK, queries)
        total = total[:, :SUB] + total[:, SUB:]
        total = total + pltpu.roll(total, rows, 1)
        width = queries // quarters
        low = iota((count, SUB, width), 1) < rows
        pieces = [
            jnp.where(
                low,
                total[:, :, 2 * i * width : (2 * i + 1) * width],
                total[:, :, (2 * i + 1) * width : (2 * i + 2) * width],
            )
            for i in range(quarters // 2)
        ]
        total = jnp.concatenate(pieces, axis=1)
        mine_ref[pl.ds(start, count)] = total
        rs_send[pl.ds(start, count)] = total.astype(BF16)

        for h in halves:
            for s in range(1 if own and h == 0 else 0, PLANE):
                s_copy(peer(p, h, s)).start()

    def score_block(p):
        score(p, False, [0])
        score(p, False, [1])

    score(blocks - 1, True, [0, 1])
    each(0, blocks - 1, score_block, 2)
    rs_recv[me] = jnp.zeros(rs_recv.shape[1:], BF16)
    wait_for(rs_recv, n - 1, s_recv_sem)

    total = mine_ref[me]
    if n <= 32:
        for src in range(n):
            total = total + rs_recv[src].astype(F32)
    else:
        total = lax.fori_loop(0, n, lambda src, v: v + rs_recv[src].astype(F32), total)
    width = queries // quarters
    for s in range(quarters):
        res_ref[:, s * width : (s + 1) * width] = total[s * rows : (s + 1) * rows]

    wait_for(send_ref, n - 1, g_send_sem)
    wait_for(rs_send, n - 1, s_send_sem)


def local(n, inputs_proj, outputs_proj, lengths, owner, fisher_inv, query_grads):
    rows = inputs_proj.shape[0]
    grad = fisher_inv.shape[1]
    queries = query_grads.shape[1]
    quarters = PACK // rows
    depth = grad // quarters
    padded = -(-depth // LANES) * LANES
    f_blocks = 4
    return pl.pallas_call(
        functools.partial(kernel, n),
        out_shape=jax.ShapeDtypeStruct((rows, queries), F32),
        in_specs=[pl.BlockSpec(memory_space=pltpu.HBM)] * 6,
        out_specs=pl.BlockSpec(memory_space=pltpu.VMEM),
        scratch_shapes=[
            pltpu.SMEM(owner.shape, jnp.int32),
            pltpu.SMEM(lengths.shape, jnp.int32),
            pltpu.VMEM(inputs_proj.shape, BF16),
            pltpu.VMEM(outputs_proj.shape, BF16),
            pltpu.VMEM((grad, grad), BF16),
            pltpu.VMEM((queries, grad), BF16),
            pltpu.VMEM((inputs_proj.shape[2] // WIDE, WIDE, LANES), F32),
            pltpu.VMEM((outputs_proj.shape[2] // quarters, LANES), F32),
            pltpu.VMEM((padded, LANES), F32),
            pltpu.VMEM((quarters, padded, queries), BF16),
            pltpu.VMEM((n, PACK, padded), BF16),
            pltpu.VMEM((n, PACK, padded), BF16),
            pltpu.VMEM((n, PACK, queries // quarters), BF16),
            pltpu.VMEM((n, PACK, queries // quarters), BF16),
            pltpu.VMEM((n, PACK, queries // quarters), F32),
            pltpu.SemaphoreType.DMA((f_blocks,)),
            pltpu.SemaphoreType.DMA((5,)),
            pltpu.SemaphoreType.DMA,
            pltpu.SemaphoreType.DMA((n // PLANE,)),
            pltpu.SemaphoreType.DMA,
            pltpu.SemaphoreType.DMA,
        ],
        compiler_params=pltpu.CompilerParams(
            collective_id=0, has_side_effects=True, vmem_limit_bytes=64 * 1024 * 1024
        ),
    )(owner, lengths, inputs_proj, outputs_proj, fisher_inv, query_grads)


def solution(mesh):
    return jax.shard_map(
        functools.partial(local, mesh.shape["mod"]),
        mesh=mesh,
        in_specs=(
            P(("grp", "mod"), None, None),
            P(("grp", "mod"), None, None),
            P(("grp", "mod")),
            P(),
            P("mod", None, None),
            P("mod", None, None),
        ),
        out_specs=P(("grp", "mod"), None),
        check_vma=False,
    )
```

```python
import functools
import math

import jax
import jax.numpy as jnp
from jax import lax
from jax.experimental import pallas as pl
from jax.experimental.pallas import tpu as pltpu
from jax.sharding import PartitionSpec as P

MESH = pl.DeviceIdType.MESH
F32 = jnp.float32
BF16 = jnp.bfloat16
NT = (((1,), (1,)), ((), ()))

LANES = 128
WIDE = 256
PACK = 16
SUB = 8
BLOCK = LANES // PACK


def nt(a, b):
    return lax.dot_general(a, b, NT, preferred_element_type=F32)


def over(a, k):
    return lax.shift_right_logical(a, k.bit_length() - 1) if k & (k - 1) == 0 else a // k


def mod(a, k):
    return lax.bitwise_and(a, k - 1) if k & (k - 1) == 0 else lax.rem(a, k)


def each(low, high, body, most=16):
    if high - low <= most:
        for k in range(low, high):
            body(k)
    else:
        pl.loop(low, high)(body)


def iota(shape, dim):
    return lax.broadcasted_iota(jnp.int32, shape, dim)


def kernel(
    n,
    owner_hbm,
    len_hbm,
    in_hbm,
    out_hbm,
    f_hbm,
    q_hbm,
    res_ref,
    owner_ref,
    len_ref,
    in_ref,
    out_ref,
    f_v,
    q_v,
    it_ref,
    ot_ref,
    gt_ref,
    p_ref,
    send_ref,
    recv_ref,
    rs_send,
    rs_recv,
    mine_ref,
    f_sem,
    small_sem,
    g_send_sem,
    g_recv_sem,
    s_send_sem,
    s_recv_sem,
):
    me = lax.axis_index("mod")
    rows = in_ref.shape[0]
    grad = f_hbm.shape[1]
    queries = q_hbm.shape[1]
    seq = math.isqrt(in_ref.shape[2] * out_ref.shape[2] // grad)
    rank_in = in_ref.shape[2] // seq
    rank_out = out_ref.shape[2] // seq
    quarters = PACK // rows
    outer = rank_out // quarters
    depth = outer * rank_in
    blocks = n // BLOCK
    chunks_in = in_ref.shape[2] // WIDE
    chunks_out = out_ref.shape[2] // WIDE
    in_low = WIDE // seq
    out_low = WIDE // (seq * quarters)
    f_blocks = f_sem.shape[0]
    f_rows = grad // f_blocks
    span = rows * n

    def f_copy(b):
        where = pl.ds(b * f_rows, f_rows)
        return pltpu.make_async_copy(f_hbm.at[0, where], f_v.at[where], f_sem.at[b])

    small = [
        pltpu.make_async_copy(src, dst, small_sem.at[i])
        for i, (src, dst) in enumerate(
            (
                (owner_hbm, owner_ref),
                (len_hbm, len_ref),
                (in_hbm, in_ref),
                (out_hbm, out_ref),
                (q_hbm.at[0], q_v),
            )
        )
    ]
    for copy in small:
        copy.start()
    for b in range(f_blocks):
        f_copy(b).start()

    barrier = pltpu.get_barrier_semaphore()

    def greet(k):
        pl.semaphore_signal(
            barrier, inc=1, device_id={"mod": mod(me + k, n)}, device_id_type=MESH
        )

    each(1, n, greet)

    a = iota((WIDE, WIDE), 0)
    b = iota((WIDE, WIDE), 1)
    swap = ((over(a, in_low) == mod(b, seq)) & (mod(a, in_low) == over(b, seq))).astype(BF16)
    a = iota((out_low * seq, WIDE), 0)
    b = iota((out_low * seq, WIDE), 1)
    fold = ((over(a, seq) == over(b, seq * quarters)) & (mod(a, seq) == mod(b, seq))).astype(BF16)
    eye = (iota((LANES, LANES), 0) == iota((LANES, LANES), 1)).astype(BF16)

    gt_ref[pl.ds(depth, gt_ref.shape[0] - depth), :] = jnp.zeros(
        (gt_ref.shape[0] - depth, LANES), F32
    )
    for s in range(quarters):
        p_ref[s, pl.ds(depth, p_ref.shape[1] - depth), :] = jnp.zeros(
            (p_ref.shape[1] - depth, queries), BF16
        )

    for copy in small[:2]:
        copy.wait()

    lane = mod(iota((1, span), 1), n)
    held = jnp.zeros((1, span), jnp.int32)
    if n <= 32:
        for m in range(n):
            held = jnp.where(lane == m, owner_ref[m], held)
    else:
        held = lax.fori_loop(
            0, n, lambda m, v: jnp.where(lane == m, owner_ref[m], v), held
        )

    a = iota((LANES, WIDE), 0)
    b = iota((LANES, WIDE), 1)
    limit = jnp.zeros((LANES, WIDE), jnp.int32)
    for e in range(rows):
        limit = jnp.where(mod(a, rows) == e, len_ref[e], limit)
    live = (mod(b, seq) < limit) & (mod(over(b, seq), quarters) == over(mod(a, PACK), rows))

    for copy in small[2:4]:
        copy.wait()

    def block_at(p):
        return mod(over(me, BLOCK) + 1 + p, blocks)

    def peer(p, s):
        return block_at(p) * BLOCK + mod(me + s, BLOCK)

    def g_copy(dst):
        return pltpu.make_async_remote_copy(
            src_ref=send_ref.at[dst],
            dst_ref=recv_ref.at[me],
            send_sem=g_send_sem,
            recv_sem=g_recv_sem.at[over(me, BLOCK)],
            device_id={"mod": dst},
            device_id_type=MESH,
        )

    def s_copy(dst):
        return pltpu.make_async_remote_copy(
            src_ref=rs_send.at[dst],
            dst_ref=rs_recv.at[me],
            send_sem=s_send_sem,
            recv_sem=s_recv_sem,
            device_id={"mod": dst},
            device_id_type=MESH,
        )

    def wait_for(ref, count, sem):
        part = ref.at[pl.ds(0, count)]
        pltpu.make_async_copy(part, part, sem).wait()

    def form(p, own):
        row = iota((LANES, span), 0)
        col = iota((LANES, span), 1)
        pick = (
            (held == block_at(p) * BLOCK + over(row, PACK)) & (over(col, n) == mod(row, rows))
        ).astype(BF16)

        for c in range(chunks_out):
            x = out_ref[:, :, c * WIDE : (c + 1) * WIDE].reshape(span, WIDE)
            y = jnp.dot(pick, x, preferred_element_type=F32)
            y = jnp.where(live, y, 0.0).astype(BF16)
            ot_ref[pl.ds(c * out_low * seq, out_low * seq), :] = nt(fold, y)
        for c in range(chunks_in):
            x = in_ref[:, :, c * WIDE : (c + 1) * WIDE].reshape(span, WIDE)
            y = jnp.dot(pick, x, preferred_element_type=F32).astype(BF16)
            it_ref[c] = nt(swap, y)

        step = outer // 2
        for first in range(0, outer, step):

            acc = [jnp.zeros((in_low, LANES), F32)] * (step * chunks_in)
            for t in range(seq):
                fi = [it_ref[c, t * in_low : (t + 1) * in_low, :] for c in range(chunks_in)]
                for o in range(step):
                    fo = ot_ref[(first + o) * seq + t : (first + o) * seq + t + 1, :]
                    for c in range(chunks_in):
                        acc[o * chunks_in + c] = acc[o * chunks_in + c] + fi[c] * fo
            for o in range(step):
                for c in range(chunks_in):
                    gt_ref[pl.ds((first + o) * rank_in + c * in_low, in_low), :] = acc[
                        o * chunks_in + c
                    ]

        formed = nt(eye, gt_ref[...].astype(BF16)).astype(BF16)
        send_ref[pl.ds(block_at(p) * BLOCK, BLOCK)] = formed.reshape(
            BLOCK, PACK, formed.shape[1]
        )

        if isinstance(p, int):
            if p == 0:
                pl.semaphore_wait(barrier, n - 1)
        else:
            pl.when(p == 0)(lambda: pl.semaphore_wait(barrier, n - 1))
        if own:
            each(1, BLOCK, lambda s: g_copy(peer(p, s)).start())
        else:
            each(0, BLOCK, lambda s: g_copy(peer(p, s)).start())

    each(0, blocks - 1, lambda p: form(p, False), 2)
    form(blocks - 1, True)
    recv_ref[me] = send_ref[me]

    small[4].wait()
    for blk in range(f_blocks):
        f_copy(blk).wait()
        part = nt(f_v[blk * f_rows : (blk + 1) * f_rows, :], q_v[...]).astype(BF16)
        for o in range(f_rows // rank_in):
            whole = blk * (f_rows // rank_in) + o
            p_ref[whole % quarters, pl.ds((whole // quarters) * rank_in, rank_in), :] = part[
                o * rank_in : (o + 1) * rank_in
            ]

    def score(p, own):
        wait_for(recv_ref, BLOCK - 1 if own else BLOCK, g_recv_sem.at[block_at(p)])
        got = recv_ref[pl.ds(block_at(p) * BLOCK, BLOCK)].reshape(LANES, p_ref.shape[1])
        row = iota(got.shape, 0)
        total = jnp.zeros((LANES, queries), F32)
        for s in range(quarters):
            mine = (over(mod(row, PACK), rows) == s).astype(F32).astype(BF16)
            total = total + jnp.dot(got * mine, p_ref[s], preferred_element_type=F32)
        total = total.reshape(BLOCK, PACK, queries)
        total = total[:, :SUB] + total[:, SUB:]
        total = total + pltpu.roll(total, rows, 1)
        width = queries // quarters
        low = iota((BLOCK, SUB, width), 1) < rows
        pieces = [
            jnp.where(
                low,
                total[:, :, 2 * i * width : (2 * i + 1) * width],
                total[:, :, (2 * i + 1) * width : (2 * i + 2) * width],
            )
            for i in range(quarters // 2)
        ]
        total = jnp.concatenate(pieces, axis=1)
        mine_ref[pl.ds(block_at(p) * BLOCK, BLOCK)] = total
        rs_send[pl.ds(block_at(p) * BLOCK, BLOCK)] = total.astype(BF16)

        if own:
            each(1, BLOCK, lambda s: s_copy(peer(p, s)).start())
        else:
            each(0, BLOCK, lambda s: s_copy(peer(p, s)).start())

    score(blocks - 1, True)
    each(0, blocks - 1, lambda p: score(p, False), 2)
    rs_recv[me] = jnp.zeros(rs_recv.shape[1:], BF16)
    wait_for(rs_recv, n - 1, s_recv_sem)

    total = mine_ref[me]
    if n <= 32:
        for src in range(n):
            total = total + rs_recv[src].astype(F32)
    else:
        total = lax.fori_loop(0, n, lambda src, v: v + rs_recv[src].astype(F32), total)
    width = queries // quarters
    for s in range(quarters):
        res_ref[:, s * width : (s + 1) * width] = total[s * rows : (s + 1) * rows]

    wait_for(send_ref, n - 1, g_send_sem)
    wait_for(rs_send, n - 1, s_send_sem)


def local(n, inputs_proj, outputs_proj, lengths, owner, fisher_inv, query_grads):
    rows = inputs_proj.shape[0]
    grad = fisher_inv.shape[1]
    queries = query_grads.shape[1]
    quarters = PACK // rows
    depth = grad // quarters
    padded = -(-depth // LANES) * LANES
    f_blocks = 1
    return pl.pallas_call(
        functools.partial(kernel, n),
        out_shape=jax.ShapeDtypeStruct((rows, queries), F32),
        in_specs=[pl.BlockSpec(memory_space=pltpu.HBM)] * 6,
        out_specs=pl.BlockSpec(memory_space=pltpu.VMEM),
        scratch_shapes=[
            pltpu.SMEM(owner.shape, jnp.int32),
            pltpu.SMEM(lengths.shape, jnp.int32),
            pltpu.VMEM(inputs_proj.shape, BF16),
            pltpu.VMEM(outputs_proj.shape, BF16),
            pltpu.VMEM((grad, grad), BF16),
            pltpu.VMEM((queries, grad), BF16),
            pltpu.VMEM((inputs_proj.shape[2] // WIDE, WIDE, LANES), F32),
            pltpu.VMEM((outputs_proj.shape[2] // quarters, LANES), F32),
            pltpu.VMEM((padded, LANES), F32),
            pltpu.VMEM((quarters, padded, queries), BF16),
            pltpu.VMEM((n, PACK, padded), BF16),
            pltpu.VMEM((n, PACK, padded), BF16),
            pltpu.VMEM((n, PACK, queries // quarters), BF16),
            pltpu.VMEM((n, PACK, queries // quarters), BF16),
            pltpu.VMEM((n, PACK, queries // quarters), F32),
            pltpu.SemaphoreType.DMA((f_blocks,)),
            pltpu.SemaphoreType.DMA((5,)),
            pltpu.SemaphoreType.DMA,
            pltpu.SemaphoreType.DMA((n // BLOCK,)),
            pltpu.SemaphoreType.DMA,
            pltpu.SemaphoreType.DMA,
        ],
        compiler_params=pltpu.CompilerParams(
            collective_id=0, has_side_effects=True, vmem_limit_bytes=64 * 1024 * 1024
        ),
    )(owner, lengths, inputs_proj, outputs_proj, fisher_inv, query_grads)


def solution(mesh):
    return jax.shard_map(
        functools.partial(local, mesh.shape["mod"]),
        mesh=mesh,
        in_specs=(
            P(("grp", "mod"), None, None),
            P(("grp", "mod"), None, None),
            P(("grp", "mod")),
            P(),
            P("mod", None, None),
            P("mod", None, None),
        ),
        out_specs=P(("grp", "mod"), None),
        check_vma=False,
    )
```

```python
import functools
import math

import jax
import jax.numpy as jnp
from jax import lax
from jax.experimental import pallas as pl
from jax.experimental.pallas import tpu as pltpu
from jax.sharding import PartitionSpec as P

MESH = pl.DeviceIdType.MESH
F32 = jnp.float32
BF16 = jnp.bfloat16
NT = (((1,), (1,)), ((), ()))

LANES = 128
WIDE = 256
PACK = 16
SUB = 8
BLOCK = LANES // PACK


def nt(a, b):
    return lax.dot_general(a, b, NT, preferred_element_type=F32)


def over(a, k):
    return lax.shift_right_logical(a, k.bit_length() - 1) if k & (k - 1) == 0 else a // k


def mod(a, k):
    return lax.bitwise_and(a, k - 1) if k & (k - 1) == 0 else lax.rem(a, k)


def each(low, high, body, most=16):
    if high - low <= most:
        for k in range(low, high):
            body(k)
    else:
        pl.loop(low, high)(body)


def iota(shape, dim):
    return lax.broadcasted_iota(jnp.int32, shape, dim)


def kernel(
    n,
    owner_hbm,
    len_hbm,
    in_hbm,
    out_hbm,
    f_hbm,
    q_hbm,
    res_ref,
    owner_ref,
    len_ref,
    in_ref,
    out_ref,
    f_v,
    q_v,
    it_ref,
    ot_ref,
    gt_ref,
    p_ref,
    send_ref,
    recv_ref,
    rs_send,
    rs_recv,
    mine_ref,
    f_sem,
    small_sem,
    g_send_sem,
    g_recv_sem,
    s_send_sem,
    s_recv_sem,
):
    me = lax.axis_index("mod")
    rows = in_ref.shape[0]
    grad = f_hbm.shape[1]
    queries = q_hbm.shape[1]
    seq = math.isqrt(in_ref.shape[2] * out_ref.shape[2] // grad)
    rank_in = in_ref.shape[2] // seq
    rank_out = out_ref.shape[2] // seq
    quarters = PACK // rows
    outer = rank_out // quarters
    depth = outer * rank_in
    blocks = n // BLOCK
    chunks_in = in_ref.shape[2] // WIDE
    chunks_out = out_ref.shape[2] // WIDE
    in_low = WIDE // seq
    out_low = WIDE // (seq * quarters)
    f_blocks = f_sem.shape[0]
    f_rows = grad // f_blocks
    span = rows * n

    def f_copy(b):
        where = pl.ds(b * f_rows, f_rows)
        return pltpu.make_async_copy(f_hbm.at[0, where], f_v.at[where], f_sem.at[b])

    small = [
        pltpu.make_async_copy(src, dst, small_sem.at[i])
        for i, (src, dst) in enumerate(
            (
                (owner_hbm, owner_ref),
                (len_hbm, len_ref),
                (in_hbm, in_ref),
                (out_hbm, out_ref),
                (q_hbm.at[0], q_v),
            )
        )
    ]
    for copy in small:
        copy.start()
    for b in range(f_blocks):
        f_copy(b).start()

    barrier = pltpu.get_barrier_semaphore()

    def greet(k):
        pl.semaphore_signal(
            barrier, inc=1, device_id={"mod": mod(me + k, n)}, device_id_type=MESH
        )

    each(1, n, greet)

    a = iota((WIDE, WIDE), 0)
    b = iota((WIDE, WIDE), 1)
    swap = ((over(a, in_low) == mod(b, seq)) & (mod(a, in_low) == over(b, seq))).astype(BF16)
    a = iota((out_low * seq, WIDE), 0)
    b = iota((out_low * seq, WIDE), 1)
    fold = ((over(a, seq) == over(b, seq * quarters)) & (mod(a, seq) == mod(b, seq))).astype(BF16)
    eye = (iota((LANES, LANES), 0) == iota((LANES, LANES), 1)).astype(BF16)

    gt_ref[pl.ds(depth, gt_ref.shape[0] - depth), :] = jnp.zeros(
        (gt_ref.shape[0] - depth, LANES), F32
    )
    for s in range(quarters):
        p_ref[s, pl.ds(depth, p_ref.shape[1] - depth), :] = jnp.zeros(
            (p_ref.shape[1] - depth, queries), BF16
        )

    for copy in small[:2]:
        copy.wait()

    lane = mod(iota((1, span), 1), n)
    held = jnp.zeros((1, span), jnp.int32)
    if n <= 32:
        for m in range(n):
            held = jnp.where(lane == m, owner_ref[m], held)
    else:
        held = lax.fori_loop(
            0, n, lambda m, v: jnp.where(lane == m, owner_ref[m], v), held
        )

    a = iota((LANES, WIDE), 0)
    b = iota((LANES, WIDE), 1)
    limit = jnp.zeros((LANES, WIDE), jnp.int32)
    for e in range(rows):
        limit = jnp.where(mod(a, rows) == e, len_ref[e], limit)
    live = (mod(b, seq) < limit) & (mod(over(b, seq), quarters) == over(mod(a, PACK), rows))

    for copy in small[2:4]:
        copy.wait()

    def block_at(p):
        return mod(over(me, BLOCK) + 1 + p, blocks)

    def peer(p, s):
        return block_at(p) * BLOCK + mod(me + s, BLOCK)

    def g_copy(dst):
        return pltpu.make_async_remote_copy(
            src_ref=send_ref.at[dst],
            dst_ref=recv_ref.at[me],
            send_sem=g_send_sem,
            recv_sem=g_recv_sem.at[over(me, BLOCK)],
            device_id={"mod": dst},
            device_id_type=MESH,
        )

    def s_copy(dst):
        return pltpu.make_async_remote_copy(
            src_ref=rs_send.at[dst],
            dst_ref=rs_recv.at[me],
            send_sem=s_send_sem,
            recv_sem=s_recv_sem,
            device_id={"mod": dst},
            device_id_type=MESH,
        )

    def wait_for(ref, count, sem):
        part = ref.at[pl.ds(0, count)]
        pltpu.make_async_copy(part, part, sem).wait()

    def precondition(half):
        cols = pl.ds(half * (queries // 2), queries // 2)
        part = nt(f_v[...], q_v[cols, :]).astype(BF16)
        for o in range(rank_out):
            p_ref[o % quarters, pl.ds((o // quarters) * rank_in, rank_in), cols] = part[
                o * rank_in : (o + 1) * rank_in
            ]

    def form(p, own):
        if own:
            small[4].wait()
            f_copy(0).wait()
        row = iota((LANES, span), 0)
        col = iota((LANES, span), 1)
        pick = (
            (held == block_at(p) * BLOCK + over(row, PACK)) & (over(col, n) == mod(row, rows))
        ).astype(BF16)

        for c in range(chunks_out):
            x = out_ref[:, :, c * WIDE : (c + 1) * WIDE].reshape(span, WIDE)
            y = jnp.dot(pick, x, preferred_element_type=F32)
            y = jnp.where(live, y, 0.0).astype(BF16)
            ot_ref[pl.ds(c * out_low * seq, out_low * seq), :] = nt(fold, y)
        for c in range(chunks_in):
            x = in_ref[:, :, c * WIDE : (c + 1) * WIDE].reshape(span, WIDE)
            y = jnp.dot(pick, x, preferred_element_type=F32).astype(BF16)
            it_ref[c] = nt(swap, y)

        step = outer // 2
        if own:
            precondition(0)
        for first in range(0, outer, step):

            acc = [jnp.zeros((in_low, LANES), F32)] * (step * chunks_in)
            for t in range(seq):
                fi = [it_ref[c, t * in_low : (t + 1) * in_low, :] for c in range(chunks_in)]
                for o in range(step):
                    fo = ot_ref[(first + o) * seq + t : (first + o) * seq + t + 1, :]
                    for c in range(chunks_in):
                        acc[o * chunks_in + c] = acc[o * chunks_in + c] + fi[c] * fo
            for o in range(step):
                for c in range(chunks_in):
                    gt_ref[pl.ds((first + o) * rank_in + c * in_low, in_low), :] = acc[
                        o * chunks_in + c
                    ]

        formed = nt(eye, gt_ref[...].astype(BF16)).astype(BF16)
        send_ref[pl.ds(block_at(p) * BLOCK, BLOCK)] = formed.reshape(
            BLOCK, PACK, formed.shape[1]
        )

        if isinstance(p, int):
            if p == 0:
                pl.semaphore_wait(barrier, n - 1)
        else:
            pl.when(p == 0)(lambda: pl.semaphore_wait(barrier, n - 1))
        if own:
            each(1, BLOCK, lambda s: g_copy(peer(p, s)).start())
        else:
            each(0, BLOCK, lambda s: g_copy(peer(p, s)).start())

    each(0, blocks - 1, lambda p: form(p, False), 2)
    form(blocks - 1, True)
    recv_ref[me] = send_ref[me]

    precondition(1)

    def score(p, own):
        wait_for(recv_ref, BLOCK - 1 if own else BLOCK, g_recv_sem.at[block_at(p)])
        got = recv_ref[pl.ds(block_at(p) * BLOCK, BLOCK)].reshape(LANES, p_ref.shape[1])
        row = iota(got.shape, 0)
        total = jnp.zeros((LANES, queries), F32)
        for s in range(quarters):
            mine = (over(mod(row, PACK), rows) == s).astype(F32).astype(BF16)
            total = total + jnp.dot(got * mine, p_ref[s], preferred_element_type=F32)
        total = total.reshape(BLOCK, PACK, queries)
        total = total[:, :SUB] + total[:, SUB:]
        total = total + pltpu.roll(total, rows, 1)
        width = queries // quarters
        low = iota((BLOCK, SUB, width), 1) < rows
        pieces = [
            jnp.where(
                low,
                total[:, :, 2 * i * width : (2 * i + 1) * width],
                total[:, :, (2 * i + 1) * width : (2 * i + 2) * width],
            )
            for i in range(quarters // 2)
        ]
        total = jnp.concatenate(pieces, axis=1)
        mine_ref[pl.ds(block_at(p) * BLOCK, BLOCK)] = total
        rs_send[pl.ds(block_at(p) * BLOCK, BLOCK)] = total.astype(BF16)

        if own:
            each(1, BLOCK, lambda s: s_copy(peer(p, s)).start())
        else:
            each(0, BLOCK, lambda s: s_copy(peer(p, s)).start())

    score(blocks - 1, True)
    each(0, blocks - 1, lambda p: score(p, False), 2)
    rs_recv[me] = jnp.zeros(rs_recv.shape[1:], BF16)
    wait_for(rs_recv, n - 1, s_recv_sem)

    total = mine_ref[me]
    if n <= 32:
        for src in range(n):
            total = total + rs_recv[src].astype(F32)
    else:
        total = lax.fori_loop(0, n, lambda src, v: v + rs_recv[src].astype(F32), total)
    width = queries // quarters
    for s in range(quarters):
        res_ref[:, s * width : (s + 1) * width] = total[s * rows : (s + 1) * rows]

    wait_for(send_ref, n - 1, g_send_sem)
    wait_for(rs_send, n - 1, s_send_sem)


def local(n, inputs_proj, outputs_proj, lengths, owner, fisher_inv, query_grads):
    rows = inputs_proj.shape[0]
    grad = fisher_inv.shape[1]
    queries = query_grads.shape[1]
    quarters = PACK // rows
    depth = grad // quarters
    padded = -(-depth // LANES) * LANES
    f_blocks = 1
    return pl.pallas_call(
        functools.partial(kernel, n),
        out_shape=jax.ShapeDtypeStruct((rows, queries), F32),
        in_specs=[pl.BlockSpec(memory_space=pltpu.HBM)] * 6,
        out_specs=pl.BlockSpec(memory_space=pltpu.VMEM),
        scratch_shapes=[
            pltpu.SMEM(owner.shape, jnp.int32),
            pltpu.SMEM(lengths.shape, jnp.int32),
            pltpu.VMEM(inputs_proj.shape, BF16),
            pltpu.VMEM(outputs_proj.shape, BF16),
            pltpu.VMEM((grad, grad), BF16),
            pltpu.VMEM((queries, grad), BF16),
            pltpu.VMEM((inputs_proj.shape[2] // WIDE, WIDE, LANES), F32),
            pltpu.VMEM((outputs_proj.shape[2] // quarters, LANES), F32),
            pltpu.VMEM((padded, LANES), F32),
            pltpu.VMEM((quarters, padded, queries), BF16),
            pltpu.VMEM((n, PACK, padded), BF16),
            pltpu.VMEM((n, PACK, padded), BF16),
            pltpu.VMEM((n, PACK, queries // quarters), BF16),
            pltpu.VMEM((n, PACK, queries // quarters), BF16),
            pltpu.VMEM((n, PACK, queries // quarters), F32),
            pltpu.SemaphoreType.DMA((f_blocks,)),
            pltpu.SemaphoreType.DMA((5,)),
            pltpu.SemaphoreType.DMA,
            pltpu.SemaphoreType.DMA((n // BLOCK,)),
            pltpu.SemaphoreType.DMA,
            pltpu.SemaphoreType.DMA,
        ],
        compiler_params=pltpu.CompilerParams(
            collective_id=0, has_side_effects=True, vmem_limit_bytes=64 * 1024 * 1024
        ),
    )(owner, lengths, inputs_proj, outputs_proj, fisher_inv, query_grads)


def solution(mesh):
    return jax.shard_map(
        functools.partial(local, mesh.shape["mod"]),
        mesh=mesh,
        in_specs=(
            P(("grp", "mod"), None, None),
            P(("grp", "mod"), None, None),
            P(("grp", "mod")),
            P(),
            P("mod", None, None),
            P("mod", None, None),
        ),
        out_specs=P(("grp", "mod"), None),
        check_vma=False,
    )
```

```python
import functools
import math

import jax
import jax.numpy as jnp
from jax import lax
from jax.experimental import pallas as pl
from jax.experimental.pallas import tpu as pltpu
from jax.sharding import PartitionSpec as P

MESH = pl.DeviceIdType.MESH
F32 = jnp.float32
BF16 = jnp.bfloat16
NT = (((1,), (1,)), ((), ()))

LANES = 128
WIDE = 256
PACK = 16
SUB = 8
BLOCK = LANES // PACK


def nt(a, b):
    return lax.dot_general(a, b, NT, preferred_element_type=F32)


def over(a, k):
    return lax.shift_right_logical(a, k.bit_length() - 1) if k & (k - 1) == 0 else a // k


def mod(a, k):
    return lax.bitwise_and(a, k - 1) if k & (k - 1) == 0 else lax.rem(a, k)


def each(low, high, body, most=16):
    if high - low <= most:
        for k in range(low, high):
            body(k)
    else:
        pl.loop(low, high)(body)


def iota(shape, dim):
    return lax.broadcasted_iota(jnp.int32, shape, dim)


def kernel(
    n,
    owner_hbm,
    len_hbm,
    in_hbm,
    out_hbm,
    f_hbm,
    q_hbm,
    res_ref,
    owner_ref,
    len_ref,
    in_ref,
    out_ref,
    f_v,
    q_v,
    it_ref,
    ot_ref,
    gt_ref,
    p_ref,
    send_ref,
    recv_ref,
    rs_send,
    rs_recv,
    mine_ref,
    f_sem,
    small_sem,
    g_send_sem,
    g_recv_sem,
    s_send_sem,
    s_recv_sem,
):
    me = lax.axis_index("mod")
    rows = in_ref.shape[0]
    grad = f_hbm.shape[1]
    queries = q_hbm.shape[1]
    seq = math.isqrt(in_ref.shape[2] * out_ref.shape[2] // grad)
    rank_in = in_ref.shape[2] // seq
    rank_out = out_ref.shape[2] // seq
    quarters = PACK // rows
    outer = rank_out // quarters
    depth = outer * rank_in
    blocks = n // BLOCK
    chunks_in = in_ref.shape[2] // WIDE
    chunks_out = out_ref.shape[2] // WIDE
    in_low = WIDE // seq
    out_low = WIDE // (seq * quarters)
    f_blocks = f_sem.shape[0]
    f_rows = grad // f_blocks
    span = rows * n

    def f_copy(b):
        where = pl.ds(b * f_rows, f_rows)
        return pltpu.make_async_copy(f_hbm.at[0, where], f_v.at[where], f_sem.at[b])

    small = [
        pltpu.make_async_copy(src, dst, small_sem.at[i])
        for i, (src, dst) in enumerate(
            (
                (owner_hbm, owner_ref),
                (len_hbm, len_ref),
                (in_hbm, in_ref),
                (out_hbm, out_ref),
            )
        )
    ]
    q_rows = queries // 4
    for i in range(4):
        where = pl.ds(i * q_rows, q_rows)
        small.append(
            pltpu.make_async_copy(q_hbm.at[0, where], q_v.at[where], small_sem.at[4 + i])
        )
    for copy in small:
        copy.start()
    for b in range(f_blocks):
        f_copy(b).start()

    barrier = pltpu.get_barrier_semaphore()

    def greet(k):
        pl.semaphore_signal(
            barrier, inc=1, device_id={"mod": mod(me + k, n)}, device_id_type=MESH
        )

    each(1, n, greet)

    a = iota((WIDE, WIDE), 0)
    b = iota((WIDE, WIDE), 1)
    swap = ((over(a, in_low) == mod(b, seq)) & (mod(a, in_low) == over(b, seq))).astype(BF16)
    a = iota((out_low * seq, WIDE), 0)
    b = iota((out_low * seq, WIDE), 1)
    fold = ((over(a, seq) == over(b, seq * quarters)) & (mod(a, seq) == mod(b, seq))).astype(BF16)
    eye = (iota((LANES, LANES), 0) == iota((LANES, LANES), 1)).astype(BF16)

    gt_ref[pl.ds(depth, gt_ref.shape[0] - depth), :] = jnp.zeros(
        (gt_ref.shape[0] - depth, LANES), F32
    )
    for s in range(quarters):
        p_ref[s, pl.ds(depth, p_ref.shape[1] - depth), :] = jnp.zeros(
            (p_ref.shape[1] - depth, queries), BF16
        )

    for copy in small[:2]:
        copy.wait()

    lane = mod(iota((1, span), 1), n)
    held = jnp.zeros((1, span), jnp.int32)
    if n <= 32:
        for m in range(n):
            held = jnp.where(lane == m, owner_ref[m], held)
    else:
        held = lax.fori_loop(
            0, n, lambda m, v: jnp.where(lane == m, owner_ref[m], v), held
        )

    a = iota((LANES, WIDE), 0)
    b = iota((LANES, WIDE), 1)
    limit = jnp.zeros((LANES, WIDE), jnp.int32)
    for e in range(rows):
        limit = jnp.where(mod(a, rows) == e, len_ref[e], limit)
    live = (mod(b, seq) < limit) & (mod(over(b, seq), quarters) == over(mod(a, PACK), rows))

    for copy in small[2:4]:
        copy.wait()

    def block_at(p):
        return mod(over(me, BLOCK) + 1 + p, blocks)

    def peer(p, s):
        return block_at(p) * BLOCK + mod(me + s, BLOCK)

    def g_copy(dst):
        return pltpu.make_async_remote_copy(
            src_ref=send_ref.at[dst],
            dst_ref=recv_ref.at[me],
            send_sem=g_send_sem,
            recv_sem=g_recv_sem.at[over(me, BLOCK)],
            device_id={"mod": dst},
            device_id_type=MESH,
        )

    def s_copy(dst):
        return pltpu.make_async_remote_copy(
            src_ref=rs_send.at[dst],
            dst_ref=rs_recv.at[me],
            send_sem=s_send_sem,
            recv_sem=s_recv_sem,
            device_id={"mod": dst},
            device_id_type=MESH,
        )

    def wait_for(ref, count, sem):
        part = ref.at[pl.ds(0, count)]
        pltpu.make_async_copy(part, part, sem).wait()

    def form(p, own):
        row = iota((LANES, span), 0)
        col = iota((LANES, span), 1)
        pick = (
            (held == block_at(p) * BLOCK + over(row, PACK)) & (over(col, n) == mod(row, rows))
        ).astype(BF16)

        for c in range(chunks_out):
            x = out_ref[:, :, c * WIDE : (c + 1) * WIDE].reshape(span, WIDE)
            y = jnp.dot(pick, x, preferred_element_type=F32)
            y = jnp.where(live, y, 0.0).astype(BF16)
            ot_ref[pl.ds(c * out_low * seq, out_low * seq), :] = nt(fold, y)
        for c in range(chunks_in):
            x = in_ref[:, :, c * WIDE : (c + 1) * WIDE].reshape(span, WIDE)
            y = jnp.dot(pick, x, preferred_element_type=F32).astype(BF16)
            it_ref[c] = nt(swap, y)

        step = outer // 2
        for first in range(0, outer, step):

            acc = [jnp.zeros((in_low, LANES), F32)] * (step * chunks_in)
            for t in range(seq):
                fi = [it_ref[c, t * in_low : (t + 1) * in_low, :] for c in range(chunks_in)]
                for o in range(step):
                    fo = ot_ref[(first + o) * seq + t : (first + o) * seq + t + 1, :]
                    for c in range(chunks_in):
                        acc[o * chunks_in + c] = acc[o * chunks_in + c] + fi[c] * fo
            for o in range(step):
                for c in range(chunks_in):
                    gt_ref[pl.ds((first + o) * rank_in + c * in_low, in_low), :] = acc[
                        o * chunks_in + c
                    ]

        formed = nt(eye, gt_ref[...].astype(BF16)).astype(BF16)
        send_ref[pl.ds(block_at(p) * BLOCK, BLOCK)] = formed.reshape(
            BLOCK, PACK, formed.shape[1]
        )

        if isinstance(p, int):
            if p == 0:
                pl.semaphore_wait(barrier, n - 1)
        else:
            pl.when(p == 0)(lambda: pl.semaphore_wait(barrier, n - 1))
        if own:
            each(1, BLOCK, lambda s: g_copy(peer(p, s)).start())
        else:
            each(0, BLOCK, lambda s: g_copy(peer(p, s)).start())

    each(0, blocks - 1, lambda p: form(p, False), 2)
    form(blocks - 1, True)
    recv_ref[me] = send_ref[me]

    for copy in small[4:]:
        copy.wait()
    for blk in range(f_blocks):
        f_copy(blk).wait()
    part = nt(f_v[...], q_v[...]).astype(BF16)
    for o in range(rank_out):
        p_ref[o % quarters, pl.ds((o // quarters) * rank_in, rank_in), :] = part[
            o * rank_in : (o + 1) * rank_in
        ]

    def score(p, own):
        wait_for(recv_ref, BLOCK - 1 if own else BLOCK, g_recv_sem.at[block_at(p)])
        got = recv_ref[pl.ds(block_at(p) * BLOCK, BLOCK)].reshape(LANES, p_ref.shape[1])
        row = iota(got.shape, 0)
        total = jnp.zeros((LANES, queries), F32)
        for s in range(quarters):
            mine = (over(mod(row, PACK), rows) == s).astype(F32).astype(BF16)
            total = total + jnp.dot(got * mine, p_ref[s], preferred_element_type=F32)
        total = total.reshape(BLOCK, PACK, queries)
        total = total[:, :SUB] + total[:, SUB:]
        total = total + pltpu.roll(total, rows, 1)
        width = queries // quarters
        low = iota((BLOCK, SUB, width), 1) < rows
        pieces = [
            jnp.where(
                low,
                total[:, :, 2 * i * width : (2 * i + 1) * width],
                total[:, :, (2 * i + 1) * width : (2 * i + 2) * width],
            )
            for i in range(quarters // 2)
        ]
        total = jnp.concatenate(pieces, axis=1)
        mine_ref[pl.ds(block_at(p) * BLOCK, BLOCK)] = total
        rs_send[pl.ds(block_at(p) * BLOCK, BLOCK)] = total.astype(BF16)

        if own:
            each(1, BLOCK, lambda s: s_copy(peer(p, s)).start())
        else:
            each(0, BLOCK, lambda s: s_copy(peer(p, s)).start())

    score(blocks - 1, True)
    each(0, blocks - 1, lambda p: score(p, False), 2)
    rs_recv[me] = jnp.zeros(rs_recv.shape[1:], BF16)
    wait_for(rs_recv, n - 1, s_recv_sem)

    total = mine_ref[me]
    if n <= 32:
        for src in range(n):
            total = total + rs_recv[src].astype(F32)
    else:
        total = lax.fori_loop(0, n, lambda src, v: v + rs_recv[src].astype(F32), total)
    width = queries // quarters
    for s in range(quarters):
        res_ref[:, s * width : (s + 1) * width] = total[s * rows : (s + 1) * rows]

    wait_for(send_ref, n - 1, g_send_sem)
    wait_for(rs_send, n - 1, s_send_sem)


def local(n, inputs_proj, outputs_proj, lengths, owner, fisher_inv, query_grads):
    rows = inputs_proj.shape[0]
    grad = fisher_inv.shape[1]
    queries = query_grads.shape[1]
    quarters = PACK // rows
    depth = grad // quarters
    padded = -(-depth // LANES) * LANES
    f_blocks = 8
    return pl.pallas_call(
        functools.partial(kernel, n),
        out_shape=jax.ShapeDtypeStruct((rows, queries), F32),
        in_specs=[pl.BlockSpec(memory_space=pltpu.HBM)] * 6,
        out_specs=pl.BlockSpec(memory_space=pltpu.VMEM),
        scratch_shapes=[
            pltpu.SMEM(owner.shape, jnp.int32),
            pltpu.SMEM(lengths.shape, jnp.int32),
            pltpu.VMEM(inputs_proj.shape, BF16),
            pltpu.VMEM(outputs_proj.shape, BF16),
            pltpu.VMEM((grad, grad), BF16),
            pltpu.VMEM((queries, grad), BF16),
            pltpu.VMEM((inputs_proj.shape[2] // WIDE, WIDE, LANES), F32),
            pltpu.VMEM((outputs_proj.shape[2] // quarters, LANES), F32),
            pltpu.VMEM((padded, LANES), F32),
            pltpu.VMEM((quarters, padded, queries), BF16),
            pltpu.VMEM((n, PACK, padded), BF16),
            pltpu.VMEM((n, PACK, padded), BF16),
            pltpu.VMEM((n, PACK, queries // quarters), BF16),
            pltpu.VMEM((n, PACK, queries // quarters), BF16),
            pltpu.VMEM((n, PACK, queries // quarters), F32),
            pltpu.SemaphoreType.DMA((f_blocks,)),
            pltpu.SemaphoreType.DMA((4 + 4,)),
            pltpu.SemaphoreType.DMA,
            pltpu.SemaphoreType.DMA((n // BLOCK,)),
            pltpu.SemaphoreType.DMA,
            pltpu.SemaphoreType.DMA,
        ],
        compiler_params=pltpu.CompilerParams(
            collective_id=0, has_side_effects=True, vmem_limit_bytes=64 * 1024 * 1024
        ),
    )(owner, lengths, inputs_proj, outputs_proj, fisher_inv, query_grads)


def solution(mesh):
    return jax.shard_map(
        functools.partial(local, mesh.shape["mod"]),
        mesh=mesh,
        in_specs=(
            P(("grp", "mod"), None, None),
            P(("grp", "mod"), None, None),
            P(("grp", "mod")),
            P(),
            P("mod", None, None),
            P("mod", None, None),
        ),
        out_specs=P(("grp", "mod"), None),
        check_vma=False,
    )
```
